32 devices in a mesh: leaf: 32 (over z, y, x, core).
Axes of the slice: x: 2, y: 2, z: 4, core: 2. Of those that a mesh axis runs over, the one named last changes fastest.
Arguments:
- points: bfloat16 [262144, 128], P('leaf'), may hold values from -6 to 6
- leaf_basis: bfloat16 [4096, 64, 32], P('leaf'), may hold values from -0.75 to 0.75
- local_transfer: bfloat16 [8160, 32, 32], P('leaf'), may hold values from -0.75 to 0.75
- top_transfer: bfloat16 [32, 32, 32], replicated, may hold values from -0.75 to 0.75
- local_coupling: bfloat16 [8160, 8, 32, 32], P('leaf'), may hold values from -0.375 to 0.375
- local_lists: int32 [8160, 8], P('leaf'), may hold values from -1 to 4095, as said below
- top_coupling: bfloat16 [32, 8, 32, 32], replicated, may hold values from -0.375 to 0.375
- top_lists: int32 [32, 8], replicated, may hold values from -1 to 31, as said below
- near_blocks: bfloat16 [4096, 6, 64, 64], P('leaf'), may hold values from -0.3125 to 0.3125
- near_lists: int32 [4096, 6], P('leaf'), may hold values from -1 to 4095, as said below
Outputs:
- product: bfloat16 [262144, 128], P('leaf')
The draws below stay inside these ranges and needn't reach their ends.
Inputs may be any that keep to these rules, and one draw needn't show every extreme that they name: `local_lists`: space is cut into 32 slabs one leaf box thick, subtree d being slab d; inside a slab the tree halves the cross-section alternately along its two directions, and a node at depth TD + k is a cell of that level's grid. Partners are children of the node's parent's neighbouring cells (in slabs d - 1, d, d + 1) that are not adjacent to the node; they are distinct within a row, and rows at depths TD to TD + 2 are empty. `top_lists`: rows of nodes at depths 0 and 1 are empty; other partners are distinct nodes of the same depth, two or more positions away from the node. `near_lists`: slot 0 is the leaf itself; the others are distinct leaves whose boxes touch the leaf's box, in the leaf's own slab or the slabs beside it.
All inputs are finite; a program needn't handle non-finite values.
Results may differ from the reference program's by a relative error of at most 0.028.
Values may be sent and summed in bfloat16 or wider, within the bound.
A program may use at most 192 MiB of HBM per device.

```python
import jax
import jax.numpy as jnp

LEAF = 64
RANK = 32
NV = 128
LEVELS_DEV = 7
ADM = 8
TOP_ADM = 8
NEAR = 6
LEAF_DEV = 128
LEAVES = 4096
POINTS = 262144
N_LEAF = 32


def depth_of(values, most):
    depth_now = jnp.zeros_like(values)
    for bit_pos in range(1, most + 1):
        depth_now = depth_now + (values >= 2 ** bit_pos).astype(jnp.int32)
    return depth_now


def cell_of(node_pos, depth_now, most):
    cell_y = jnp.zeros_like(node_pos)
    cell_z = jnp.zeros_like(node_pos)
    for step_pos in range(1, most + 1):
        active = step_pos <= depth_now
        shift_by = jnp.maximum(depth_now - step_pos, 0).astype(jnp.int32)
        bit_now = jnp.right_shift(node_pos, shift_by) & 1
        if step_pos % 2 == 1:
            cell_y = jnp.where(active, cell_y * 2 + bit_now, cell_y)
        else:
            cell_z = jnp.where(active, cell_z * 2 + bit_now, cell_z)
    return (cell_y, cell_z)


def node_of(cell_y, cell_z, depth_now, most):
    bits_y = (depth_now + 1) // 2
    bits_z = depth_now // 2
    node_pos = jnp.zeros_like(cell_y)
    for step_pos in range(1, most + 1):
        active = step_pos <= depth_now
        if step_pos % 2 == 1:
            shift_by = jnp.maximum(bits_y - (step_pos + 1) // 2, 0).astype(jnp.int32)
            bit_now = jnp.right_shift(cell_y, shift_by) & 1
        else:
            shift_by = jnp.maximum(bits_z - step_pos // 2, 0).astype(jnp.int32)
            bit_now = jnp.right_shift(cell_z, shift_by) & 1
        node_pos = jnp.where(active, node_pos * 2 + bit_now, node_pos)
    return node_pos


def distinct(chosen, valid):
    columns = []
    for slot_idx in range(chosen.shape[1]):
        keep = valid[:, slot_idx]
        for prior in range(slot_idx):
            keep = keep & ((chosen[:, slot_idx] != chosen[:, prior]) | ~valid[:, prior])
        columns.append(keep)
    keep_all = jnp.stack(columns, axis=1)
    return jnp.where(keep_all, chosen, -1).astype(jnp.int32)


def draw_local_lists(key, part):
    key = jax.random.fold_in(key, 11)
    nodes_dev = 2 * LEAF_DEV - 1
    row_count = N_LEAF * nodes_dev
    row_ids = jnp.arange(row_count, dtype=jnp.int32)
    device_ids = (row_ids // nodes_dev)[:, None]
    heap_pos = row_ids % nodes_dev + 1
    depth_now = depth_of(heap_pos, LEVELS_DEV)[:, None]
    node_pos = heap_pos[:, None] - jnp.left_shift(1, depth_now)
    cell_y, cell_z = cell_of(node_pos, depth_now, LEVELS_DEV)
    parent_depth = jnp.maximum(depth_now - 1, 0)
    par_y, par_z = cell_of(node_pos // 2, parent_depth, LEVELS_DEV)
    par_ny = jnp.left_shift(1, (parent_depth + 1) // 2)
    par_nz = jnp.left_shift(1, parent_depth // 2)
    key_slab, key_y, key_z, key_child = jax.random.split(key, 4)
    shape_now = (row_count, ADM)
    slab_step = jax.random.randint(key_slab, shape_now, -1, 2)
    slot_ids = jnp.arange(ADM, dtype=jnp.int32)[None, :]
    slab_step = jnp.where(slot_ids == 0, jnp.where(device_ids < N_LEAF - 1, 1, -1), slab_step)
    slab_step = jnp.where(slot_ids == 1, jnp.where(device_ids > 0, -1, 1), slab_step)
    other_dev = device_ids + slab_step
    other_py = par_y + jax.random.randint(key_y, shape_now, -1, 2)
    other_pz = par_z + jax.random.randint(key_z, shape_now, -1, 2)
    child_bit = jax.random.randint(key_child, shape_now, 0, 2)
    other_pos = 2 * node_of(jnp.clip(other_py, 0, par_ny - 1), jnp.clip(other_pz, 0, par_nz - 1), parent_depth, LEVELS_DEV) + child_bit
    other_y, other_z = cell_of(other_pos, depth_now, LEVELS_DEV)
    apart = jnp.maximum(jnp.abs(other_y - cell_y), jnp.abs(other_z - cell_z)) >= 2
    valid = (depth_now >= 3) & (other_dev >= 0) & (other_dev < N_LEAF)
    valid = valid & (other_py >= 0) & (other_py < par_ny) & (other_pz >= 0) & (other_pz < par_nz) & apart
    chosen = other_dev * jnp.left_shift(1, depth_now) + other_pos
    return distinct(chosen, valid)


def draw_top_lists(key, part):
    key = jax.random.fold_in(key, 23)
    node_ids = jnp.arange(N_LEAF, dtype=jnp.int32)
    depth_now = depth_of(jnp.maximum(node_ids, 1), 12)
    spread = jnp.left_shift(1, depth_now).astype(jnp.int32)
    half_way = spread + (node_ids - spread + spread // 2) % spread
    raw_pick = jax.random.randint(key, (N_LEAF, TOP_ADM), 0, 1 << 30)
    chosen = spread[:, None] + raw_pick % spread[:, None]
    slot_ids = jnp.arange(TOP_ADM, dtype=jnp.int32)[None, :]
    chosen = jnp.where(slot_ids == 0, half_way[:, None], chosen)
    valid = (jnp.abs(chosen - node_ids[:, None]) >= 2) & (depth_now[:, None] >= 2)
    return distinct(chosen, valid)


def draw_near_lists(key, part):
    key = jax.random.fold_in(key, 37)
    leaf_ids = jnp.arange(LEAVES, dtype=jnp.int32)[:, None]
    device_ids = leaf_ids // LEAF_DEV
    leaf_pos = leaf_ids % LEAF_DEV
    cell_y, cell_z = cell_of(leaf_pos, LEVELS_DEV, LEVELS_DEV)
    grid_y = 2 ** ((LEVELS_DEV + 1) // 2)
    grid_z = 2 ** (LEVELS_DEV // 2)
    key_slab, key_y, key_z = jax.random.split(key, 3)
    shape_now = (LEAVES, NEAR)
    slot_ids = jnp.arange(NEAR, dtype=jnp.int32)[None, :]
    slab_step = jax.random.randint(key_slab, shape_now, -1, 2)
    step_y = jax.random.randint(key_y, shape_now, -1, 2)
    step_z = jax.random.randint(key_z, shape_now, -1, 2)
    slab_step = jnp.where(slot_ids == 1, jnp.where(device_ids > 0, -1, 1), slab_step)
    step_y = jnp.where(slot_ids <= 1, 0, step_y)
    step_z = jnp.where(slot_ids <= 1, 0, step_z)
    slab_step = jnp.where(slot_ids == 0, 0, slab_step)
    other_dev = device_ids + slab_step
    other_y = cell_y + step_y
    other_z = cell_z + step_z
    valid = (other_dev >= 0) & (other_dev < N_LEAF) & (other_y >= 0) & (other_y < grid_y) & (other_z >= 0) & (other_z < grid_z)
    other_pos = node_of(jnp.clip(other_y, 0, grid_y - 1), jnp.clip(other_z, 0, grid_z - 1), LEVELS_DEV, LEVELS_DEV)
    chosen = other_dev * LEAF_DEV + other_pos
    return distinct(chosen, valid)


def block_levels(rng, dims, cuts, least, high):
    def one(position, parts):
        draws = jax.random.uniform(jax.random.fold_in(jax.random.fold_in(rng, 6), position), (parts,), jnp.float32, least / len(cuts), high / len(cuts))
        return jnp.repeat(jnp.exp(draws), dims[position] // parts).reshape((-1,) + (1,) * (len(dims) - position - 1))

    loudness = one(*cuts[0])
    for cut in cuts[1:]:
        loudness = loudness * one(*cut)
    return loudness


def gaussian(rng, dims, width, bound, cuts=(), held_as=jnp.bfloat16):
    factor_of = block_levels(rng, dims, cuts, -0.22, 0.18) if cuts else 1.0
    drawn = jax.random.normal(rng, dims, jnp.float32) * width * factor_of
    return jnp.minimum(jnp.maximum(drawn, -bound), bound).astype(held_as)


def setup_inputs(seed: int = 0) -> dict:
    key_of = jax.random.split(jax.random.key(seed), 11)
    points = gaussian(key_of[0], (POINTS, NV), 1.0, 6.0, ((0, 32),))
    leaf_basis = gaussian(key_of[1], (LEAVES, LEAF, RANK), LEAF ** -0.5, 0.75, ((0, 32),))
    local_transfer = gaussian(key_of[2], (N_LEAF * (2 * LEAF_DEV - 1), RANK, RANK), (2 * RANK) ** -0.5, 0.75, ((0, 32),))
    top_transfer = gaussian(key_of[3], (N_LEAF, RANK, RANK), (2 * RANK) ** -0.5, 0.75)
    local_coupling = gaussian(key_of[4], (N_LEAF * (2 * LEAF_DEV - 1), ADM, RANK, RANK), (ADM * RANK) ** -0.5, 0.375, ((0, 32),))
    local_lists = draw_local_lists(jax.random.fold_in(key_of[10], 71), 0)
    top_coupling = gaussian(key_of[6], (N_LEAF, TOP_ADM, RANK, RANK), (TOP_ADM * RANK) ** -0.5, 0.375)
    top_lists = draw_top_lists(jax.random.fold_in(key_of[10], 71), 0)
    near_blocks = gaussian(key_of[8], (LEAVES, NEAR, LEAF, LEAF), (NEAR * LEAF) ** -0.5, 0.3125, ((0, 32),))
    near_lists = draw_near_lists(jax.random.fold_in(key_of[10], 71), 0)
    return {"points": points, "leaf_basis": leaf_basis, "local_transfer": local_transfer, "top_transfer": top_transfer, "local_coupling": local_coupling, "local_lists": local_lists, "top_coupling": top_coupling, "top_lists": top_lists, "near_blocks": near_blocks, "near_lists": near_lists}


def couple(coeff_level, blocks, partner_ids, first_node):
    is_valid = partner_ids >= 0
    positions = jnp.where(is_valid, partner_ids - first_node, 0).astype(jnp.int32)
    total = jnp.zeros((blocks.shape[0], blocks.shape[2], coeff_level.shape[2]), jnp.float32)
    for slot_idx in range(partner_ids.shape[1]):
        picked = coeff_level[positions[:, slot_idx]].astype(jnp.float32)
        picked = jnp.where(is_valid[:, slot_idx, None, None], picked, jnp.float32(0.0))
        total = total + jnp.einsum('mrs,msv->mrv', blocks[:, slot_idx].astype(jnp.float32), picked)
    return total


def reference(points, leaf_basis, local_transfer, top_transfer, local_coupling, local_lists, top_coupling, top_lists, near_blocks, near_lists):
    top_depth = N_LEAF.bit_length() - 1
    nodes_dev = 2 * LEAF_DEV - 1
    leaf_rows = points.reshape(LEAVES, LEAF, NV)
    shaped_transfer = local_transfer.reshape(N_LEAF, nodes_dev, RANK, RANK)
    shaped_coupling = local_coupling.reshape(N_LEAF, nodes_dev, ADM, RANK, RANK)
    shaped_lists = local_lists.reshape(N_LEAF, nodes_dev, ADM)

    def at_depth(array, depth_now):
        lower = 2 ** depth_now - 1
        return array[:, lower:2 * lower + 1].reshape((-1,) + array.shape[2:])

    coeffs = [None] * (LEVELS_DEV + 1)
    coeffs[LEVELS_DEV] = jnp.einsum('lpr,lpv->lrv', leaf_basis.astype(jnp.float32), leaf_rows.astype(jnp.float32)).astype(jnp.bfloat16)
    for depth_now in range(LEVELS_DEV - 1, -1, -1):
        transfers = at_depth(shaped_transfer, depth_now + 1).astype(jnp.float32)
        up_terms = jnp.einsum('crs,crv->csv', transfers, coeffs[depth_now + 1].astype(jnp.float32))
        coeffs[depth_now] = up_terms.reshape(-1, 2, RANK, NV).sum(axis=1).astype(jnp.bfloat16)
    up_terms = jnp.einsum('crs,crv->csv', at_depth(shaped_transfer, 0).astype(jnp.float32), coeffs[0].astype(jnp.float32))
    top_coeffs = {}
    for depth_now in range(top_depth - 1, 1, -1):
        level_coeff = up_terms.reshape(-1, 2, RANK, NV).sum(axis=1).astype(jnp.bfloat16)
        top_coeffs[depth_now] = level_coeff
        if depth_now > 2:
            transfers = top_transfer[2 ** depth_now:2 ** (depth_now + 1)].astype(jnp.float32)
            up_terms = jnp.einsum('crs,crv->csv', transfers, level_coeff.astype(jnp.float32))
    carried = None
    for depth_now in range(2, top_depth):
        lower = 2 ** depth_now
        far_now = couple(top_coeffs[depth_now], top_coupling[lower:2 * lower], top_lists[lower:2 * lower], lower)
        if carried is None:
            carried = far_now
        else:
            parents = jnp.repeat(carried.astype(jnp.bfloat16), 2, axis=0).astype(jnp.float32)
            carried = far_now + jnp.einsum('crs,csv->crv', top_transfer[lower:2 * lower].astype(jnp.float32), parents)
    for depth_now in range(0, LEVELS_DEV + 1):
        far_now = couple(coeffs[depth_now], at_depth(shaped_coupling, depth_now), at_depth(shaped_lists, depth_now), 0)
        parents = jnp.repeat(carried.astype(jnp.bfloat16), 2, axis=0).astype(jnp.float32)
        carried = far_now + jnp.einsum('crs,csv->crv', at_depth(shaped_transfer, depth_now).astype(jnp.float32), parents)
    far_rows = jnp.einsum('lpr,lrv->lpv', leaf_basis.astype(jnp.float32), carried.astype(jnp.bfloat16).astype(jnp.float32))
    near_rows = couple(leaf_rows, near_blocks, near_lists, 0)
    return (far_rows + near_rows).astype(jnp.bfloat16).reshape(POINTS, NV)
```

```python
import functools

import jax
import jax.numpy as jnp
from jax import lax
from jax.experimental import pallas as pl
from jax.experimental.pallas import tpu as pltpu
from jax.sharding import PartitionSpec as P

BF = jnp.bfloat16
F32 = jnp.float32
VMEM = pl.BlockSpec(memory_space=pltpu.VMEM)
SMEM = pl.BlockSpec(memory_space=pltpu.SMEM)
PARAMS = pltpu.CompilerParams(vmem_limit_bytes=56 * 1024 * 1024)


def mask_of(rows, cols, row_block, col_block):
    row = lax.broadcasted_iota(jnp.int32, (rows, cols), 0) // row_block
    col = lax.broadcasted_iota(jnp.int32, (rows, cols), 1) // col_block
    return jnp.where(row == col, 1.0, 0.0).astype(BF)


def dot(a, b):
    return jnp.dot(a, b, preferred_element_type=F32)


def rows_at(start, size):
    if isinstance(start, int):
        return pl.ds(start, size)
    return pl.ds(pl.multiple_of(start, 32), size)


def spread(group, mask):
    return jnp.concatenate([group] * 4, axis=0) * mask


def up_pass(x_ref, g_ref, dst_ref, level_rows, rank, leaf_dev, lowest):
    mask = mask_of(4 * rank, 256, rank, 64)
    depth = leaf_dev.bit_length() - 1
    groups = leaf_dev // 4

    def leaves(i, carry):
        out = dot(spread(g_ref[i], mask), x_ref[rows_at(i * 256, 256), :])
        dst_ref[rows_at(level_rows[depth] + i * 128, 128), :] = out.astype(BF)
        return carry

    lax.fori_loop(0, groups, leaves, 0, unroll=4)
    for k in range(depth - 1, lowest - 1, -1):
        count = 2**k // 4
        base = groups + 2 ** (k + 1) // 8 - 2

        def nodes(i, carry, k=k, base=base):
            src = dst_ref[rows_at(level_rows[k + 1] + i * 256, 256), :]
            out = dot(spread(g_ref[base + i], mask), src)
            dst_ref[rows_at(level_rows[k] + i * 128, 128), :] = out.astype(BF)
            return carry

        lax.fori_loop(0, count, nodes, 0, unroll=min(4, count))


def own_kernel(rank, leaf_dev, x_ref, g_ref, low_ref, coeff_ref, root_ref):
    depth = leaf_dev.bit_length() - 1
    level_rows = {k: (2**k - 8) * rank for k in range(3, depth + 1)}
    up_pass(x_ref, g_ref, coeff_ref, level_rows, rank, leaf_dev, 3)
    mask = mask_of(4 * rank, 256, rank, 64)
    state = coeff_ref[0:256, :]
    zeros = jnp.zeros((128, state.shape[1]), BF)
    for step in range(4):
        out = dot(spread(low_ref[step], mask), state)
        if step < 3:
            state = jnp.concatenate([out.astype(BF), zeros], axis=0)
    root_ref[...] = out[0:rank, :]


def top_kernel(rank, top_depth, pos_ref, g_ref, up_ref, s_ref, e_ref, low_ref, out_ref, win):
    up_mask = mask_of(4 * rank, 256, rank, 64)
    count = 2 ** (top_depth - 1)
    for i in range(count):
        pair = g_ref[2 * i * rank : (2 * i + 1) * rank, :]
        other = g_ref[(2 * i + 1) * rank : (2 * i + 2) * rank, :]
        win[(count + i) * rank : (count + i + 1) * rank, :] = (pair + other).astype(BF)
    for k in range(top_depth - 2, 1, -1):
        for i in range(2**k // 4):
            src = win[(2 ** (k + 1)) * rank + i * 256 : (2 ** (k + 1)) * rank + (i + 1) * 256, :]
            out = dot(spread(up_ref[2 ** (k + 1) // 8 - 1 + i], up_mask), src)
            win[2**k * rank + i * 128 : 2**k * rank + (i + 1) * 128, :] = out.astype(BF)
    win[0:rank, :] = jnp.zeros((rank, win.shape[1]), BF)
    carried = None
    slots = s_ref.shape[2] // rank
    for j in range(top_depth - 2):
        parts = [
            win[rows_at(pos_ref[j * slots + s] * rank, rank), :] for s in range(slots)
        ]
        far = dot(s_ref[j], jnp.concatenate(parts, axis=0))
        if carried is not None:
            far = far + dot(e_ref[j], carried)
        carried = far.astype(BF)
    state = dot(low_ref[0:rank, 0:rank], carried).astype(BF)
    first = dot(low_ref[rank : 3 * rank, 0:rank], state).astype(BF)
    halves = [
        dot(low_ref[(3 + 2 * i) * rank : (5 + 2 * i) * rank, 0:rank], first[i * rank : (i + 1) * rank])
        for i in range(2)
    ]
    out_ref[...] = jnp.concatenate(halves, axis=0).astype(BF)


def near_kernel(leaf_dev, size, pos_ref, b_ref, xb_ref, xo_ref, xa_ref, out_ref, win, sems):
    copies = []
    rows = leaf_dev * size
    for i, src in enumerate((xb_ref, xo_ref, xa_ref)):
        copies.append(pltpu.make_async_copy(src, win.at[pl.ds(i * rows, rows)], sems.at[i]))
        copies[-1].start()
    win[3 * rows : 3 * rows + size, :] = jnp.zeros((size, win.shape[1]), BF)
    for copy in copies:
        copy.wait()
    slots = b_ref.shape[2] // size

    def leaf(l, carry):
        parts = [
            win[pl.ds(pl.multiple_of(pos_ref[l * slots + s] * size, size), size), :]
            for s in range(slots)
        ]
        out_ref[pl.ds(pl.multiple_of(l * size, size), size), :] = dot(
            b_ref[l], jnp.concatenate(parts, axis=0)
        )
        return carry

    lax.fori_loop(0, leaf_dev, leaf, 0, unroll=4)


def far_kernel(
    rank,
    leaf_dev,
    pos_ref,
    xb_ref,
    xa_ref,
    gb_ref,
    ga_ref,
    coeff_ref,
    s_ref,
    e_ref,
    basis_ref,
    down_ref,
    near_ref,
    out_ref,
    win,
    down,
):
    depth = leaf_dev.bit_length() - 1
    offset = {k: 3 * (2**k - 8) * rank for k in range(3, depth + 1)}
    for k in range(3, depth + 1):
        size = 2**k * rank
        win[offset[k] + size : offset[k] + 2 * size, :] = coeff_ref[
            (2**k - 8) * rank : (2**k - 8) * rank + size, :
        ]
    total = 3 * (2 ** (depth + 1) - 8) * rank
    win[total : total + rank, :] = jnp.zeros((rank, win.shape[1]), BF)
    up_pass(xb_ref, gb_ref, win, offset, rank, leaf_dev, 3)
    after = {k: offset[k] + 2 * 2**k * rank for k in offset}
    up_pass(xa_ref, ga_ref, win, after, rank, leaf_dev, 3)
    mask = mask_of(256, 128, 64, 32)
    slots = s_ref.shape[2] // rank
    down[0:128, :] = down_ref[...]
    for k in range(3, depth + 1):

        def group(i, carry, k=k):
            parents = down[rows_at((2 ** (k - 1) - 4) * rank + i * 128, 128), :]
            base = (2**k - 8) + i * 8
            total_now = dot(e_ref[rows_at(base * rank, 256), :] * mask, parents)
            fars = []
            for j in range(8):
                node = base + j
                parts = [
                    win[rows_at(pos_ref[node * slots + s] * rank, rank), :] for s in range(slots)
                ]
                fars.append(dot(s_ref[node], jnp.concatenate(parts, axis=0)))
            total_now = total_now + jnp.concatenate(fars, axis=0)
            down[rows_at((2**k - 4) * rank + i * 256, 256), :] = total_now.astype(BF)
            return carry

        lax.fori_loop(0, 2**k // 8, group, 0)

    def leaves(i, carry):
        state = down[rows_at((2**depth - 4) * rank + i * 128, 128), :]
        here = rows_at(i * 256, 256)
        out = near_ref[here, :] + dot(basis_ref[here, :] * mask, state)
        out_ref[here, :] = out.astype(BF)
        return carry

    lax.fori_loop(0, leaf_dev // 4, leaves, 0, unroll=2)


def grouped_up(transfer):
    count, rank = transfer.shape[0], transfer.shape[1]
    return transfer.reshape(count // 8, 8, rank, rank).transpose(0, 3, 1, 2).reshape(-1, rank, 8 * rank)


def shards(
    points,
    leaf_basis,
    local_transfer,
    top_transfer,
    local_coupling,
    local_lists,
    top_coupling,
    top_lists,
    near_blocks,
    near_lists,
):
    leaf_dev, size, rank = leaf_basis.shape
    vecs = points.shape[1]
    depth = leaf_dev.bit_length() - 1
    devices = lax.axis_size("leaf")
    top_depth = devices.bit_length() - 1
    own = lax.axis_index("leaf")
    up = [(i, i + 1) for i in range(devices - 1)]
    back = [(i + 1, i) for i in range(devices - 1)]

    x_before = lax.ppermute(points, "leaf", up)
    x_after = lax.ppermute(points, "leaf", back)
    basis_up = (
        leaf_basis.reshape(leaf_dev // 4, 4, size, rank)
        .transpose(0, 3, 1, 2)
        .reshape(leaf_dev // 4, rank, 4 * size)
    )
    g_own = jnp.concatenate([basis_up, grouped_up(local_transfer[15:])], axis=0)
    g_before = lax.ppermute(g_own, "leaf", up)
    g_after = lax.ppermute(g_own, "leaf", back)

    def padded(rows):
        flat = rows.transpose(2, 0, 1).reshape(rank, -1)
        return jnp.pad(flat, ((0, 0), (0, 256 - flat.shape[1])))

    low_up = jnp.stack(
        [padded(local_transfer[a:b]) for a, b in ((7, 15), (3, 7), (1, 3), (0, 1))]
    )
    nodes = 2 * leaf_dev - 8
    coeff_own, root_term = pl.pallas_call(
        functools.partial(own_kernel, rank, leaf_dev),
        out_shape=(
            jax.ShapeDtypeStruct((nodes * rank, vecs), BF),
            jax.ShapeDtypeStruct((rank, vecs), F32),
        ),
        in_specs=[VMEM] * 3,
        out_specs=(VMEM, VMEM),
        compiler_params=PARAMS,
        cost_estimate=pl.CostEstimate(flops=600_000_000, bytes_accessed=5_000_000, transcendentals=0),
        name="own_up",
    )(points, g_own, low_up)
    gathered = lax.all_gather(root_term, "leaf", axis=0, tiled=True)

    steps = jnp.arange(2, top_depth)
    ancestors = (devices + own) >> (top_depth - steps)
    lists = top_lists[ancestors]
    top_pos = jnp.where(lists >= 0, lists, 0).reshape(-1)
    s_top = top_coupling[ancestors].transpose(0, 2, 1, 3).reshape(top_depth - 2, rank, -1)
    e_top = top_transfer[ancestors]
    low_down = local_transfer[:8].reshape(8 * rank, rank)
    down_two = pl.pallas_call(
        functools.partial(top_kernel, rank, top_depth),
        out_shape=jax.ShapeDtypeStruct((4 * rank, vecs), BF),
        in_specs=[SMEM] + [VMEM] * 5,
        out_specs=VMEM,
        scratch_shapes=[pltpu.VMEM((devices * rank, vecs), BF)],
        compiler_params=PARAMS,
        cost_estimate=pl.CostEstimate(flops=50_000_000, bytes_accessed=1_000_000, transcendentals=0),
        name="top_tree",
    )(top_pos, gathered, grouped_up(top_transfer[8:]), s_top, e_top, low_down)

    first_leaf = (own - 1) * leaf_dev
    near_pos = jnp.where(near_lists >= 0, near_lists - first_leaf, 3 * leaf_dev).reshape(-1)
    near_cat = near_blocks.transpose(0, 2, 1, 3).reshape(leaf_dev, size, -1)
    near_rows = pl.pallas_call(
        functools.partial(near_kernel, leaf_dev, size),
        out_shape=jax.ShapeDtypeStruct((leaf_dev * size, vecs), F32),
        in_specs=[SMEM, VMEM] + [pl.BlockSpec(memory_space=pl.ANY)] * 3,
        out_specs=VMEM,
        scratch_shapes=[
            pltpu.VMEM(((3 * leaf_dev + 1) * size, vecs), BF),
            pltpu.SemaphoreType.DMA((3,)),
        ],
        compiler_params=PARAMS,
        cost_estimate=pl.CostEstimate(
            flops=2_000_000_000, bytes_accessed=20_000_000, transcendentals=0
        ),
        name="near_field",
    )(near_pos, near_cat, x_before, points, x_after)

    far_lists = local_lists[7:]
    row = jnp.arange(7, 2 * leaf_dev - 1)
    width = jnp.zeros_like(row)
    for k in range(3, depth + 1):
        width = jnp.where(row >= 2**k - 1, 2**k, width)
    start = 3 * (width - 8) - (own - 1) * width
    far_pos = jnp.where(far_lists >= 0, far_lists + start[:, None], 3 * nodes).reshape(-1)
    s_cat = local_coupling[7:].transpose(0, 2, 1, 3).reshape(nodes, rank, -1)
    e_tiled = jnp.tile(local_transfer[7:], (1, 1, 4)).reshape(nodes * rank, 4 * rank)
    basis_tiled = jnp.tile(leaf_basis, (1, 1, 4)).reshape(leaf_dev * size, 4 * rank)
    return pl.pallas_call(
        functools.partial(far_kernel, rank, leaf_dev),
        out_shape=jax.ShapeDtypeStruct((leaf_dev * size, vecs), BF),
        in_specs=[SMEM] + [VMEM] * 10,
        out_specs=VMEM,
        scratch_shapes=[
            pltpu.VMEM(((3 * nodes + 1) * rank, vecs), BF),
            pltpu.VMEM(((nodes + 4) * rank, vecs), BF),
        ],
        compiler_params=PARAMS,
        cost_estimate=pl.CostEstimate(
            flops=2_000_000_000, bytes_accessed=20_000_000, transcendentals=0
        ),
        name="far_field",
    )(
        far_pos,
        x_before,
        x_after,
        g_before,
        g_after,
        coeff_own,
        s_cat,
        e_tiled,
        basis_tiled,
        down_two,
        near_rows,
    )


def solution(mesh):
    return jax.shard_map(
        shards,
        mesh=mesh,
        in_specs=(
            P("leaf", None),
            P("leaf", None, None),
            P("leaf", None, None),
            P(),
            P("leaf", None, None, None),
            P("leaf", None),
            P(),
            P(),
            P("leaf", None, None, None),
            P("leaf", None),
        ),
        out_specs=P("leaf", None),
        check_vma=False,
    )
```

```python
import functools

import jax
import jax.numpy as jnp
from jax import lax
from jax.experimental import pallas as pl
from jax.experimental.pallas import tpu as pltpu
from jax.sharding import PartitionSpec as P

BF = jnp.bfloat16
F32 = jnp.float32
VMEM = pl.BlockSpec(memory_space=pltpu.VMEM)
SMEM = pl.BlockSpec(memory_space=pltpu.SMEM)
PARAMS = pltpu.CompilerParams(vmem_limit_bytes=56 * 1024 * 1024)


def mask_of(rows, cols, row_block, col_block):
    row = lax.broadcasted_iota(jnp.int32, (rows, cols), 0) // row_block
    col = lax.broadcasted_iota(jnp.int32, (rows, cols), 1) // col_block
    return jnp.where(row == col, 1.0, 0.0).astype(BF)


def dot(a, b):
    return jnp.dot(a, b, preferred_element_type=F32)


def rows_at(start, size):
    if isinstance(start, int):
        return pl.ds(start, size)
    return pl.ds(pl.multiple_of(start, 32), size)


def spread(group, mask):
    return jnp.concatenate([group] * 4, axis=0) * mask


def up_pass(sides, dst_ref, rank, leaf_dev):
    mask = mask_of(4 * rank, 256, rank, 64)
    depth = leaf_dev.bit_length() - 1
    groups = leaf_dev // 4

    def leaves(i, carry):
        for x_ref, first, g_ref, level_rows in sides:
            out = dot(spread(g_ref[i], mask), x_ref[rows_at(first + i * 256, 256), :])
            dst_ref[rows_at(level_rows[depth] + i * 128, 128), :] = out.astype(BF)
        return carry

    lax.fori_loop(0, groups, leaves, 0, unroll=4)
    for k in range(depth - 1, 2, -1):
        count = 2**k // 4
        base = groups + 2 ** (k + 1) // 8 - 2

        def nodes(i, carry, k=k, base=base):
            for _, _, g_ref, level_rows in sides:
                src = dst_ref[rows_at(level_rows[k + 1] + i * 256, 256), :]
                out = dot(spread(g_ref[base + i], mask), src)
                dst_ref[rows_at(level_rows[k] + i * 128, 128), :] = out.astype(BF)
            return carry

        lax.fori_loop(0, count, nodes, 0, unroll=min(4, count))


def own_kernel(rank, leaf_dev, x_ref, g_ref, low_ref, coeff_ref, root_ref):
    depth = leaf_dev.bit_length() - 1
    level_rows = {k: (2**k - 8) * rank for k in range(3, depth + 1)}
    up_pass([(x_ref, 0, g_ref, level_rows)], coeff_ref, rank, leaf_dev)
    mask = mask_of(4 * rank, 256, rank, 64)
    state = coeff_ref[0:256, :]
    zeros = jnp.zeros((128, state.shape[1]), BF)
    for step in range(4):
        out = dot(spread(low_ref[step], mask), state)
        if step < 3:
            state = jnp.concatenate([out.astype(BF), zeros], axis=0)
    root_ref[...] = out[0:rank, :]


def top_kernel(rank, top_depth, pos_ref, g_ref, up_ref, s_ref, e_ref, low_ref, out_ref, win):
    up_mask = mask_of(4 * rank, 256, rank, 64)
    count = 2 ** (top_depth - 1)
    win[count * rank : 2 * count * rank, :] = g_ref[...]
    for k in range(top_depth - 2, 1, -1):
        for i in range(2**k // 4):
            src = win[(2 ** (k + 1)) * rank + i * 256 : (2 ** (k + 1)) * rank + (i + 1) * 256, :]
            out = dot(spread(up_ref[2 ** (k + 1) // 8 - 1 + i], up_mask), src)
            win[2**k * rank + i * 128 : 2**k * rank + (i + 1) * 128, :] = out.astype(BF)
    win[0:rank, :] = jnp.zeros((rank, win.shape[1]), BF)
    carried = None
    slots = s_ref.shape[2] // rank
    for j in range(top_depth - 2):
        parts = [
            win[rows_at(pos_ref[j * slots + s] * rank, rank), :] for s in range(slots)
        ]
        far = dot(s_ref[j], jnp.concatenate(parts, axis=0))
        if carried is not None:
            far = far + dot(e_ref[j], carried)
        carried = far.astype(BF)
    state = dot(low_ref[0:rank, 0:rank], carried).astype(BF)
    first = dot(low_ref[rank : 3 * rank, 0:rank], state).astype(BF)
    halves = [
        dot(low_ref[(3 + 2 * i) * rank : (5 + 2 * i) * rank, 0:rank], first[i * rank : (i + 1) * rank])
        for i in range(2)
    ]
    out_ref[...] = jnp.concatenate(halves, axis=0).astype(BF)


def prep_kernel(g_ref, low_ref, e_ref, basis_ref):
    rank = g_ref.shape[1]
    mask = mask_of(4 * rank, 256, rank, 64)
    groups = basis_ref.shape[0] // 256

    def turned(group):
        return jnp.transpose(spread(group, mask))

    e_ref[0:256, :] = turned(low_ref[0])

    def bases(i, carry):
        basis_ref[rows_at(i * 256, 256), :] = turned(g_ref[i])
        return carry

    def transfers(i, carry):
        e_ref[rows_at(256 + i * 256, 256), :] = turned(g_ref[groups + i])
        return carry

    lax.fori_loop(0, groups, bases, 0, unroll=2)
    lax.fori_loop(0, g_ref.shape[0] - groups, transfers, 0, unroll=2)


def field_kernel(
    rank,
    leaf_dev,
    size,
    near_pos,
    far_pos,
    xb_hbm,
    xo_hbm,
    xa_hbm,
    gb_hbm,
    ga_hbm,
    b_hbm,
    s_hbm,
    e_hbm,
    basis_hbm,
    coeff_hbm,
    down_hbm,
    out_ref,
    xs,
    gb,
    ga,
    b_ref,
    s_ref,
    e_ref,
    basis_ref,
    win,
    down,
    sems,
):
    depth = leaf_dev.bit_length() - 1
    rows = leaf_dev * size
    offset = {k: 3 * (2**k - 8) * rank for k in range(3, depth + 1)}
    copies = []

    def begin(src, dst):
        copies.append(pltpu.make_async_copy(src, dst, sems.at[len(copies)]))
        copies[-1].start()
        return copies[-1]

    first = [
        begin(gb_hbm, gb),
        begin(ga_hbm, ga),
        begin(xb_hbm, xs.at[pl.ds(0, rows)]),
        begin(xa_hbm, xs.at[pl.ds(2 * rows, rows)]),
    ]
    second = [begin(down_hbm, down.at[pl.ds(0, 4 * rank)]), begin(s_hbm, s_ref), begin(e_hbm, e_ref)]
    for k in range(3, depth + 1):
        level = 2**k * rank
        second.append(
            begin(
                coeff_hbm.at[pl.ds((2**k - 8) * rank, level)], win.at[pl.ds(offset[k] + level, level)]
            )
        )
    third = [
        begin(xo_hbm, xs.at[pl.ds(rows, rows)]),
        begin(basis_hbm, basis_ref),
        begin(b_hbm, b_ref),
    ]
    total = 3 * (2 ** (depth + 1) - 8) * rank
    win[total : total + rank, :] = jnp.zeros((rank, win.shape[1]), BF)
    xs[3 * rows : 3 * rows + size, :] = jnp.zeros((size, xs.shape[1]), BF)
    for copy in first:
        copy.wait()
    after = {k: offset[k] + 2 * 2**k * rank for k in offset}
    up_pass([(xs, 0, gb, offset), (xs, 2 * rows, ga, after)], win, rank, leaf_dev)
    for copy in second:
        copy.wait()
    slots = s_ref.shape[2] // rank
    for k in range(3, depth + 1):

        def group(i, carry, k=k):
            parents = down[rows_at((2 ** (k - 1) - 4) * rank + i * 128, 128), :]
            base = (2**k - 8) + i * 8
            total_now = dot(e_ref[rows_at(base * rank, 256), :], parents)
            fars = []
            for j in range(8):
                node = base + j
                parts = [
                    win[rows_at(far_pos[node * slots + s] * rank, rank), :] for s in range(slots)
                ]
                fars.append(dot(s_ref[node], jnp.concatenate(parts, axis=0)))
            total_now = total_now + jnp.concatenate(fars, axis=0)
            down[rows_at((2**k - 4) * rank + i * 256, 256), :] = total_now.astype(BF)
            return carry

        lax.fori_loop(0, 2**k // 8, group, 0)
    for copy in third:
        copy.wait()
    near_slots = b_ref.shape[2] // size

    def leaves(i, carry):
        state = down[rows_at((2**depth - 4) * rank + i * 128, 128), :]
        here = rows_at(i * 256, 256)
        near = []
        for j in range(4):
            leaf = i * 4 + j
            parts = [
                xs[rows_at(near_pos[leaf * near_slots + s] * size, size), :]
                for s in range(near_slots)
            ]
            near.append(dot(b_ref[leaf], jnp.concatenate(parts, axis=0)))
        out = jnp.concatenate(near, axis=0) + dot(basis_ref[here, :], state)
        out_ref[here, :] = out.astype(BF)
        return carry

    lax.fori_loop(0, leaf_dev // 4, leaves, 0, unroll=2)


def grouped_up(transfer):
    count, rank = transfer.shape[0], transfer.shape[1]
    return transfer.reshape(count // 8, 8, rank, rank).transpose(0, 3, 1, 2).reshape(-1, rank, 8 * rank)


def shards(
    points,
    leaf_basis,
    local_transfer,
    top_transfer,
    local_coupling,
    local_lists,
    top_coupling,
    top_lists,
    near_blocks,
    near_lists,
):
    leaf_dev, size, rank = leaf_basis.shape
    vecs = points.shape[1]
    depth = leaf_dev.bit_length() - 1
    devices = lax.axis_size("leaf")
    top_depth = devices.bit_length() - 1
    own = lax.axis_index("leaf")
    up = [(i, i + 1) for i in range(devices - 1)]
    back = [(i + 1, i) for i in range(devices - 1)]

    x_before = lax.ppermute(points, "leaf", up)
    x_after = lax.ppermute(points, "leaf", back)
    basis_up = (
        leaf_basis.reshape(leaf_dev // 4, 4, size, rank)
        .transpose(0, 3, 1, 2)
        .reshape(leaf_dev // 4, rank, 4 * size)
    )
    g_own = jnp.concatenate([basis_up, grouped_up(local_transfer[15:])], axis=0)
    g_before = lax.ppermute(g_own, "leaf", up)
    g_after = lax.ppermute(g_own, "leaf", back)

    def padded(rows):
        flat = rows.transpose(2, 0, 1).reshape(rank, -1)
        return jnp.pad(flat, ((0, 0), (0, 256 - flat.shape[1])))

    low_up = jnp.stack(
        [padded(local_transfer[a:b]) for a, b in ((7, 15), (3, 7), (1, 3), (0, 1))]
    )
    nodes = 2 * leaf_dev - 8
    coeff_own, root_term = pl.pallas_call(
        functools.partial(own_kernel, rank, leaf_dev),
        out_shape=(
            jax.ShapeDtypeStruct((nodes * rank, vecs), BF),
            jax.ShapeDtypeStruct((rank, vecs), F32),
        ),
        in_specs=[VMEM] * 3,
        out_specs=(VMEM, VMEM),
        compiler_params=PARAMS,
        cost_estimate=pl.CostEstimate(flops=600_000_000, bytes_accessed=5_000_000, transcendentals=0),
        name="own_up",
    )(points, g_own, low_up)
    near_blocks, root_term = lax.optimization_barrier((near_blocks, root_term))
    other = lax.ppermute(root_term, "leaf", [(i, i ^ 1) for i in range(devices)])
    near_cat = near_blocks.transpose(0, 2, 1, 3).reshape(leaf_dev, size, -1)
    near_cat, other = lax.optimization_barrier((near_cat, other))
    gathered = (root_term + other).astype(BF)
    for bit in range(1, top_depth):
        flip = 2**bit
        if bit == 1:
            local_coupling, gathered = lax.optimization_barrier((local_coupling, gathered))
        if bit == 2:
            g_late, gathered = lax.optimization_barrier((g_own, gathered))
        other = lax.ppermute(gathered, "leaf", [(i, i ^ flip) for i in range(devices)])
        if bit == 1:
            s_cat = local_coupling[7:].transpose(0, 2, 1, 3).reshape(nodes, rank, -1)
            s_cat, other = lax.optimization_barrier((s_cat, other))
        if bit == 2:
            e_groups, basis_groups = pl.pallas_call(
                prep_kernel,
                out_shape=(
                    jax.ShapeDtypeStruct((nodes * rank, 4 * rank), BF),
                    jax.ShapeDtypeStruct((leaf_dev * size, 4 * rank), BF),
                ),
                in_specs=[VMEM] * 2,
                out_specs=(VMEM, VMEM),
                compiler_params=PARAMS,
                cost_estimate=pl.CostEstimate(flops=400_000_000, bytes_accessed=5_000_000, transcendentals=0),
                name="prepare_down",
            )(g_late, low_up)
            e_groups, basis_groups, other = lax.optimization_barrier(
                (e_groups, basis_groups, other)
            )
        upper = (own & flip) > 0
        gathered = jnp.concatenate(
            [jnp.where(upper, other, gathered), jnp.where(upper, gathered, other)], axis=0
        )

    steps = jnp.arange(2, top_depth)
    ancestors = (devices + own) >> (top_depth - steps)
    lists = top_lists[ancestors]
    top_pos = jnp.where(lists >= 0, lists, 0).reshape(-1)
    s_top = top_coupling[ancestors].transpose(0, 2, 1, 3).reshape(top_depth - 2, rank, -1)
    e_top = top_transfer[ancestors]
    low_down = local_transfer[:8].reshape(8 * rank, rank)
    down_two = pl.pallas_call(
        functools.partial(top_kernel, rank, top_depth),
        out_shape=jax.ShapeDtypeStruct((4 * rank, vecs), BF),
        in_specs=[SMEM] + [VMEM] * 5,
        out_specs=VMEM,
        scratch_shapes=[pltpu.VMEM((devices * rank, vecs), BF)],
        compiler_params=PARAMS,
        cost_estimate=pl.CostEstimate(flops=50_000_000, bytes_accessed=1_000_000, transcendentals=0),
        name="top_tree",
    )(top_pos, gathered, grouped_up(top_transfer[8:]), s_top, e_top, low_down)

    first_leaf = (own - 1) * leaf_dev
    near_pos = jnp.where(near_lists >= 0, near_lists - first_leaf, 3 * leaf_dev).reshape(-1)
    far_lists = local_lists[7:]
    row = jnp.arange(7, 2 * leaf_dev - 1)
    width = jnp.zeros_like(row)
    for k in range(3, depth + 1):
        width = jnp.where(row >= 2**k - 1, 2**k, width)
    start = 3 * (width - 8) - (own - 1) * width
    far_pos = jnp.where(far_lists >= 0, far_lists + start[:, None], 3 * nodes).reshape(-1)
    any_space = pl.BlockSpec(memory_space=pl.ANY)
    return pl.pallas_call(
        functools.partial(field_kernel, rank, leaf_dev, size),
        out_shape=jax.ShapeDtypeStruct((leaf_dev * size, vecs), BF),
        in_specs=[SMEM] * 2 + [any_space] * 11,
        out_specs=VMEM,
        scratch_shapes=[
            pltpu.VMEM(((3 * leaf_dev + 1) * size, vecs), BF),
            pltpu.VMEM(g_own.shape, BF),
            pltpu.VMEM(g_own.shape, BF),
            pltpu.VMEM(near_cat.shape, BF),
            pltpu.VMEM(s_cat.shape, BF),
            pltpu.VMEM(e_groups.shape, BF),
            pltpu.VMEM(basis_groups.shape, BF),
            pltpu.VMEM(((3 * nodes + 1) * rank, vecs), BF),
            pltpu.VMEM(((nodes + 4) * rank, vecs), BF),
            pltpu.SemaphoreType.DMA((10 + depth - 2,)),
        ],
        compiler_params=PARAMS,
        cost_estimate=pl.CostEstimate(
            flops=4_000_000_000, bytes_accessed=30_000_000, transcendentals=0
        ),
        name="near_and_far",
    )(
        near_pos,
        far_pos,
        x_before,
        points,
        x_after,
        g_before,
        g_after,
        near_cat,
        s_cat,
        e_groups,
        basis_groups,
        coeff_own,
        down_two,
    )


def solution(mesh):
    return jax.shard_map(
        shards,
        mesh=mesh,
        in_specs=(
            P("leaf", None),
            P("leaf", None, None),
            P("leaf", None, None),
            P(),
            P("leaf", None, None, None),
            P("leaf", None),
            P(),
            P(),
            P("leaf", None, None, None),
            P("leaf", None),
        ),
        out_specs=P("leaf", None),
        check_vma=False,
    )
```

```python
import functools

import jax
import jax.numpy as jnp
from jax import lax
from jax.experimental.layout import Layout, with_layout_constraint
from jax.experimental import pallas as pl
from jax.experimental.pallas import tpu as pltpu
from jax.sharding import PartitionSpec as P

BF = jnp.bfloat16
F32 = jnp.float32
VMEM = pl.BlockSpec(memory_space=pltpu.VMEM)
SMEM = pl.BlockSpec(memory_space=pltpu.SMEM)
PARAMS = pltpu.CompilerParams(vmem_limit_bytes=56 * 1024 * 1024)


def mask_of(rows, cols, row_block, col_block):
    row = lax.broadcasted_iota(jnp.int32, (rows, cols), 0) // row_block
    col = lax.broadcasted_iota(jnp.int32, (rows, cols), 1) // col_block
    return jnp.where(row == col, 1.0, 0.0).astype(BF)


def dot(a, b):
    return jnp.dot(a, b, preferred_element_type=F32)


def rows_at(start, size):
    if isinstance(start, int):
        return pl.ds(start, size)
    return pl.ds(pl.multiple_of(start, 32), size)


def spread(group, mask):
    return jnp.concatenate([group] * 4, axis=0) * mask


def up_pass(sides, dst_ref, rank, leaf_dev):
    mask = mask_of(4 * rank, 256, rank, 64)
    depth = leaf_dev.bit_length() - 1
    groups = leaf_dev // 4

    def leaves(i, carry):
        for x_ref, first, g_ref, level_rows in sides:
            out = dot(spread(g_ref[i], mask), x_ref[rows_at(first + i * 256, 256), :])
            dst_ref[rows_at(level_rows[depth] + i * 128, 128), :] = out.astype(BF)
        return carry

    lax.fori_loop(0, groups, leaves, 0, unroll=4)
    for k in range(depth - 1, 2, -1):
        count = 2**k // 4
        base = groups + 2 ** (k + 1) // 8 - 2

        def nodes(i, carry, k=k, base=base):
            for _, _, g_ref, level_rows in sides:
                src = dst_ref[rows_at(level_rows[k + 1] + i * 256, 256), :]
                out = dot(spread(g_ref[base + i], mask), src)
                dst_ref[rows_at(level_rows[k] + i * 128, 128), :] = out.astype(BF)
            return carry

        lax.fori_loop(0, count, nodes, 0, unroll=min(4, count))


def own_kernel(rank, leaf_dev, x_ref, g_ref, low_ref, coeff_ref, root_ref):
    depth = leaf_dev.bit_length() - 1
    level_rows = {k: (2**k - 8) * rank for k in range(3, depth + 1)}
    up_pass([(x_ref, 0, g_ref, level_rows)], coeff_ref, rank, leaf_dev)
    mask = mask_of(4 * rank, 256, rank, 64)
    state = coeff_ref[0:256, :]
    zeros = jnp.zeros((128, state.shape[1]), BF)
    for step in range(4):
        out = dot(spread(low_ref[step], mask), state)
        if step < 3:
            state = jnp.concatenate([out.astype(BF), zeros], axis=0)
    root_ref[...] = out[0:rank, :]


def top_kernel(rank, top_depth, pos_ref, g_ref, up_ref, s_ref, e_ref, low_ref, out_ref, win):
    up_mask = mask_of(4 * rank, 256, rank, 64)
    count = 2 ** (top_depth - 1)
    win[count * rank : 2 * count * rank, :] = g_ref[...]
    for k in range(top_depth - 2, 1, -1):
        for i in range(2**k // 4):
            src = win[(2 ** (k + 1)) * rank + i * 256 : (2 ** (k + 1)) * rank + (i + 1) * 256, :]
            out = dot(spread(up_ref[2 ** (k + 1) // 8 - 1 + i], up_mask), src)
            win[2**k * rank + i * 128 : 2**k * rank + (i + 1) * 128, :] = out.astype(BF)
    win[0:rank, :] = jnp.zeros((rank, win.shape[1]), BF)
    carried = None
    slots = s_ref.shape[2] // rank
    for j in range(top_depth - 2):
        parts = [
            win[rows_at(pos_ref[j * slots + s] * rank, rank), :] for s in range(slots)
        ]
        far = dot(s_ref[j], jnp.concatenate(parts, axis=0))
        if carried is not None:
            far = far + dot(e_ref[j], carried)
        carried = far.astype(BF)
    state = dot(low_ref[0:rank, 0:rank], carried).astype(BF)
    first = dot(low_ref[rank : 3 * rank, 0:rank], state).astype(BF)
    halves = [
        dot(low_ref[(3 + 2 * i) * rank : (5 + 2 * i) * rank, 0:rank], first[i * rank : (i + 1) * rank])
        for i in range(2)
    ]
    out_ref[...] = jnp.concatenate(halves, axis=0).astype(BF)


def prep_kernel(g_ref, low_ref, e_ref, basis_ref):
    rank = g_ref.shape[1]
    mask = mask_of(4 * rank, 256, rank, 64)
    groups = basis_ref.shape[0] // 256

    def turned(group):
        return jnp.transpose(spread(group, mask))

    e_ref[0:256, :] = turned(low_ref[0])

    def bases(i, carry):
        basis_ref[rows_at(i * 256, 256), :] = turned(g_ref[i])
        return carry

    def transfers(i, carry):
        e_ref[rows_at(256 + i * 256, 256), :] = turned(g_ref[groups + i])
        return carry

    lax.fori_loop(0, groups, bases, 0, unroll=2)
    lax.fori_loop(0, g_ref.shape[0] - groups, transfers, 0, unroll=2)


def field_kernel(
    rank,
    leaf_dev,
    size,
    near_pos,
    far_pos,
    xb_hbm,
    xo_hbm,
    xa_hbm,
    gb_hbm,
    ga_hbm,
    b_hbm,
    s_hbm,
    e_hbm,
    basis_hbm,
    coeff_hbm,
    down_hbm,
    out_ref,
    xs,
    gb,
    ga,
    b_ref,
    s_ref,
    e_ref,
    basis_ref,
    win,
    down,
    sems,
):
    depth = leaf_dev.bit_length() - 1
    rows = leaf_dev * size
    offset = {k: 3 * (2**k - 8) * rank for k in range(3, depth + 1)}
    copies = []

    def begin(src, dst):
        copies.append(pltpu.make_async_copy(src, dst, sems.at[len(copies)]))
        copies[-1].start()
        return copies[-1]

    first = [
        begin(gb_hbm, gb),
        begin(ga_hbm, ga),
        begin(xb_hbm, xs.at[pl.ds(0, rows)]),
        begin(xa_hbm, xs.at[pl.ds(2 * rows, rows)]),
    ]
    second = [begin(down_hbm, down.at[pl.ds(0, 4 * rank)]), begin(s_hbm, s_ref), begin(e_hbm, e_ref)]
    for k in range(3, depth + 1):
        level = 2**k * rank
        second.append(
            begin(
                coeff_hbm.at[pl.ds((2**k - 8) * rank, level)], win.at[pl.ds(offset[k] + level, level)]
            )
        )
    third = [
        begin(xo_hbm, xs.at[pl.ds(rows, rows)]),
        begin(basis_hbm, basis_ref),
        begin(b_hbm, b_ref),
    ]
    total = 3 * (2 ** (depth + 1) - 8) * rank
    win[total : total + rank, :] = jnp.zeros((rank, win.shape[1]), BF)
    xs[3 * rows : 3 * rows + size, :] = jnp.zeros((size, xs.shape[1]), BF)
    for copy in first:
        copy.wait()
    after = {k: offset[k] + 2 * 2**k * rank for k in offset}
    up_pass([(xs, 0, gb, offset), (xs, 2 * rows, ga, after)], win, rank, leaf_dev)
    for copy in second:
        copy.wait()
    slots = s_ref.shape[2] // rank
    for k in range(3, depth + 1):

        def group(i, carry, k=k):
            parents = down[rows_at((2 ** (k - 1) - 4) * rank + i * 128, 128), :]
            base = (2**k - 8) + i * 8
            total_now = dot(e_ref[rows_at(base * rank, 256), :], parents)
            fars = []
            for j in range(8):
                node = base + j
                parts = [
                    win[rows_at(far_pos[node * slots + s] * rank, rank), :] for s in range(slots)
                ]
                fars.append(dot(s_ref[node], jnp.concatenate(parts, axis=0)))
            total_now = total_now + jnp.concatenate(fars, axis=0)
            down[rows_at((2**k - 4) * rank + i * 256, 256), :] = total_now.astype(BF)
            return carry

        lax.fori_loop(0, 2**k // 8, group, 0)
    for copy in third:
        copy.wait()
    near_slots = b_ref.shape[2] // size

    def leaves(i, carry):
        state = down[rows_at((2**depth - 4) * rank + i * 128, 128), :]
        here = rows_at(i * 256, 256)
        near = []
        for j in range(4):
            leaf = i * 4 + j
            parts = [
                xs[rows_at(near_pos[leaf * near_slots + s] * size, size), :]
                for s in range(near_slots)
            ]
            near.append(dot(b_ref[leaf], jnp.concatenate(parts, axis=0)))
        out = jnp.concatenate(near, axis=0) + dot(basis_ref[here, :], state)
        out_ref[here, :] = out.astype(BF)
        return carry

    lax.fori_loop(0, leaf_dev // 4, leaves, 0, unroll=2)


def grouped_up(transfer):
    count, rank = transfer.shape[0], transfer.shape[1]
    return transfer.reshape(count // 8, 8, rank, rank).transpose(0, 3, 1, 2).reshape(-1, rank, 8 * rank)


def shards(
    points,
    leaf_basis,
    local_transfer,
    top_transfer,
    local_coupling,
    local_lists,
    top_coupling,
    top_lists,
    near_blocks,
    near_lists,
):
    leaf_dev, size, rank = leaf_basis.shape
    vecs = points.shape[1]
    depth = leaf_dev.bit_length() - 1
    devices = lax.axis_size("leaf")
    top_depth = devices.bit_length() - 1
    own = lax.axis_index("leaf")
    up = [(i, i + 1) for i in range(devices - 1)]
    back = [(i + 1, i) for i in range(devices - 1)]

    x_before = lax.ppermute(points, "leaf", up)
    x_after = lax.ppermute(points, "leaf", back)
    basis_up = (
        leaf_basis.reshape(leaf_dev // 4, 4, size, rank)
        .transpose(0, 3, 1, 2)
        .reshape(leaf_dev // 4, rank, 4 * size)
    )
    g_own = jnp.concatenate([basis_up, grouped_up(local_transfer[15:])], axis=0)
    g_before = lax.ppermute(g_own, "leaf", up)
    g_after = lax.ppermute(g_own, "leaf", back)

    def padded(rows):
        flat = rows.transpose(2, 0, 1).reshape(rank, -1)
        return jnp.pad(flat, ((0, 0), (0, 256 - flat.shape[1])))

    low_up = jnp.stack(
        [padded(local_transfer[a:b]) for a, b in ((7, 15), (3, 7), (1, 3), (0, 1))]
    )
    nodes = 2 * leaf_dev - 8
    coeff_own, root_term = pl.pallas_call(
        functools.partial(own_kernel, rank, leaf_dev),
        out_shape=(
            jax.ShapeDtypeStruct((nodes * rank, vecs), BF),
            jax.ShapeDtypeStruct((rank, vecs), F32),
        ),
        in_specs=[VMEM] * 3,
        out_specs=(VMEM, VMEM),
        compiler_params=PARAMS,
        cost_estimate=pl.CostEstimate(flops=600_000_000, bytes_accessed=5_000_000, transcendentals=0),
        name="own_up",
    )(points, g_own, low_up)
    other = lax.ppermute(root_term, "leaf", [(i, i ^ 1) for i in range(devices)])
    gathered = (root_term + other).astype(BF)
    for bit in range(1, top_depth):
        flip = 2**bit
        if bit == 1:
            near_blocks, local_coupling, gathered = lax.optimization_barrier(
                (near_blocks, local_coupling, gathered)
            )
        if bit == 2:
            g_late, gathered = lax.optimization_barrier((g_own, gathered))
        other = lax.ppermute(gathered, "leaf", [(i, i ^ flip) for i in range(devices)])
        if bit == 1:
            near_cat = near_blocks.transpose(0, 2, 1, 3).reshape(leaf_dev, size, -1)
            near_cat = with_layout_constraint(near_cat, Layout((0, 1, 2)))
            s_cat = local_coupling[7:].transpose(0, 2, 1, 3).reshape(nodes, rank, -1)
            s_cat = with_layout_constraint(s_cat, Layout((0, 1, 2)))
            near_cat, s_cat, other = lax.optimization_barrier((near_cat, s_cat, other))
        if bit == 2:
            e_groups, basis_groups = pl.pallas_call(
                prep_kernel,
                out_shape=(
                    jax.ShapeDtypeStruct((nodes * rank, 4 * rank), BF),
                    jax.ShapeDtypeStruct((leaf_dev * size, 4 * rank), BF),
                ),
                in_specs=[VMEM] * 2,
                out_specs=(VMEM, VMEM),
                compiler_params=PARAMS,
                cost_estimate=pl.CostEstimate(flops=400_000_000, bytes_accessed=5_000_000, transcendentals=0),
                name="prepare_down",
            )(g_late, low_up)
            e_groups, basis_groups, other = lax.optimization_barrier(
                (e_groups, basis_groups, other)
            )
        upper = (own & flip) > 0
        gathered = jnp.concatenate(
            [jnp.where(upper, other, gathered), jnp.where(upper, gathered, other)], axis=0
        )

    steps = jnp.arange(2, top_depth)
    ancestors = (devices + own) >> (top_depth - steps)
    lists = top_lists[ancestors]
    top_pos = jnp.where(lists >= 0, lists, 0).reshape(-1)
    s_top = top_coupling[ancestors].transpose(0, 2, 1, 3).reshape(top_depth - 2, rank, -1)
    e_top = top_transfer[ancestors]
    low_down = local_transfer[:8].reshape(8 * rank, rank)
    down_two = pl.pallas_call(
        functools.partial(top_kernel, rank, top_depth),
        out_shape=jax.ShapeDtypeStruct((4 * rank, vecs), BF),
        in_specs=[SMEM] + [VMEM] * 5,
        out_specs=VMEM,
        scratch_shapes=[pltpu.VMEM((devices * rank, vecs), BF)],
        compiler_params=PARAMS,
        cost_estimate=pl.CostEstimate(flops=50_000_000, bytes_accessed=1_000_000, transcendentals=0),
        name="top_tree",
    )(top_pos, gathered, grouped_up(top_transfer[8:]), s_top, e_top, low_down)

    first_leaf = (own - 1) * leaf_dev
    near_pos = jnp.where(near_lists >= 0, near_lists - first_leaf, 3 * leaf_dev).reshape(-1)
    far_lists = local_lists[7:]
    row = jnp.arange(7, 2 * leaf_dev - 1)
    width = jnp.zeros_like(row)
    for k in range(3, depth + 1):
        width = jnp.where(row >= 2**k - 1, 2**k, width)
    start = 3 * (width - 8) - (own - 1) * width
    far_pos = jnp.where(far_lists >= 0, far_lists + start[:, None], 3 * nodes).reshape(-1)
    any_space = pl.BlockSpec(memory_space=pl.ANY)
    return pl.pallas_call(
        functools.partial(field_kernel, rank, leaf_dev, size),
        out_shape=jax.ShapeDtypeStruct((leaf_dev * size, vecs), BF),
        in_specs=[SMEM] * 2 + [any_space] * 11,
        out_specs=VMEM,
        scratch_shapes=[
            pltpu.VMEM(((3 * leaf_dev + 1) * size, vecs), BF),
            pltpu.VMEM(g_own.shape, BF),
            pltpu.VMEM(g_own.shape, BF),
            pltpu.VMEM(near_cat.shape, BF),
            pltpu.VMEM(s_cat.shape, BF),
            pltpu.VMEM(e_groups.shape, BF),
            pltpu.VMEM(basis_groups.shape, BF),
            pltpu.VMEM(((3 * nodes + 1) * rank, vecs), BF),
            pltpu.VMEM(((nodes + 4) * rank, vecs), BF),
            pltpu.SemaphoreType.DMA((10 + depth - 2,)),
        ],
        compiler_params=PARAMS,
        cost_estimate=pl.CostEstimate(
            flops=4_000_000_000, bytes_accessed=30_000_000, transcendentals=0
        ),
        name="near_and_far",
    )(
        near_pos,
        far_pos,
        x_before,
        points,
        x_after,
        g_before,
        g_after,
        near_cat,
        s_cat,
        e_groups,
        basis_groups,
        coeff_own,
        down_two,
    )


def solution(mesh):
    return jax.shard_map(
        shards,
        mesh=mesh,
        in_specs=(
            P("leaf", None),
            P("leaf", None, None),
            P("leaf", None, None),
            P(),
            P("leaf", None, None, None),
            P("leaf", None),
            P(),
            P(),
            P("leaf", None, None, None),
            P("leaf", None),
        ),
        out_specs=P("leaf", None),
        check_vma=False,
    )
```

```python
import functools

import jax
import jax.numpy as jnp
from jax import lax
from jax.experimental.layout import Layout, with_layout_constraint
from jax.experimental import pallas as pl
from jax.experimental.pallas import tpu as pltpu
from jax.sharding import PartitionSpec as P

BF = jnp.bfloat16
F32 = jnp.float32
VMEM = pl.BlockSpec(memory_space=pltpu.VMEM)
SMEM = pl.BlockSpec(memory_space=pltpu.SMEM)
PARAMS = pltpu.CompilerParams(vmem_limit_bytes=56 * 1024 * 1024)


def mask_of(rows, cols, row_block, col_block):
    row = lax.broadcasted_iota(jnp.int32, (rows, cols), 0) // row_block
    col = lax.broadcasted_iota(jnp.int32, (rows, cols), 1) // col_block
    return jnp.where(row == col, 1.0, 0.0).astype(BF)


def dot(a, b):
    return jnp.dot(a, b, preferred_element_type=F32)


def rows_at(start, size):
    if isinstance(start, int):
        return pl.ds(start, size)
    return pl.ds(pl.multiple_of(start, 32), size)


def spread(group, mask):
    return jnp.concatenate([group] * 4, axis=0) * mask


def up_pass(sides, dst_ref, rank, leaf_dev):
    mask = mask_of(4 * rank, 256, rank, 64)
    depth = leaf_dev.bit_length() - 1
    groups = leaf_dev // 4

    def leaves(i, carry):
        for x_ref, first, g_ref, level_rows in sides:
            out = dot(spread(g_ref[i], mask), x_ref[rows_at(first + i * 256, 256), :])
            dst_ref[rows_at(level_rows[depth] + i * 128, 128), :] = out.astype(BF)
        return carry

    lax.fori_loop(0, groups, leaves, 0, unroll=4)
    for k in range(depth - 1, 2, -1):
        count = 2**k // 4
        base = groups + 2 ** (k + 1) // 8 - 2

        def nodes(i, carry, k=k, base=base):
            for _, _, g_ref, level_rows in sides:
                src = dst_ref[rows_at(level_rows[k + 1] + i * 256, 256), :]
                out = dot(spread(g_ref[base + i], mask), src)
                dst_ref[rows_at(level_rows[k] + i * 128, 128), :] = out.astype(BF)
            return carry

        lax.fori_loop(0, count, nodes, 0, unroll=min(4, count))


def own_kernel(rank, leaf_dev, x_ref, g_ref, low_ref, coeff_ref, root_ref):
    depth = leaf_dev.bit_length() - 1
    level_rows = {k: (2**k - 8) * rank for k in range(3, depth + 1)}
    up_pass([(x_ref, 0, g_ref, level_rows)], coeff_ref, rank, leaf_dev)
    mask = mask_of(4 * rank, 256, rank, 64)
    state = coeff_ref[0:256, :]
    zeros = jnp.zeros((128, state.shape[1]), BF)
    for step in range(4):
        out = dot(spread(low_ref[step], mask), state)
        if step < 3:
            state = jnp.concatenate([out.astype(BF), zeros], axis=0)
    root_ref[...] = out[0:rank, :]


def top_kernel(rank, top_depth, pos_ref, g_ref, up_ref, s_ref, e_ref, low_ref, out_ref, win):
    up_mask = mask_of(4 * rank, 256, rank, 64)
    count = 2 ** (top_depth - 1)
    win[count * rank : 2 * count * rank, :] = g_ref[...]
    for k in range(top_depth - 2, 1, -1):
        for i in range(2**k // 4):
            src = win[(2 ** (k + 1)) * rank + i * 256 : (2 ** (k + 1)) * rank + (i + 1) * 256, :]
            out = dot(spread(up_ref[2 ** (k + 1) // 8 - 1 + i], up_mask), src)
            win[2**k * rank + i * 128 : 2**k * rank + (i + 1) * 128, :] = out.astype(BF)
    win[0:rank, :] = jnp.zeros((rank, win.shape[1]), BF)
    carried = None
    slots = s_ref.shape[2] // rank
    for j in range(top_depth - 2):
        parts = [
            win[rows_at(pos_ref[j * slots + s] * rank, rank), :] for s in range(slots)
        ]
        far = dot(s_ref[j], jnp.concatenate(parts, axis=0))
        if carried is not None:
            far = far + dot(e_ref[j], carried)
        carried = far.astype(BF)
    state = dot(low_ref[0:rank, 0:rank], carried).astype(BF)
    first = dot(low_ref[rank : 3 * rank, 0:rank], state).astype(BF)
    halves = [
        dot(low_ref[(3 + 2 * i) * rank : (5 + 2 * i) * rank, 0:rank], first[i * rank : (i + 1) * rank])
        for i in range(2)
    ]
    out_ref[...] = jnp.concatenate(halves, axis=0).astype(BF)


def prep_kernel(g_ref, low_ref, e_ref, basis_ref):
    rank = g_ref.shape[1]
    mask = mask_of(4 * rank, 256, rank, 64)
    groups = basis_ref.shape[0] // 256

    def turned(group):
        return jnp.transpose(spread(group, mask))

    e_ref[0:256, :] = turned(low_ref[0])

    def bases(i, carry):
        basis_ref[rows_at(i * 256, 256), :] = turned(g_ref[i])
        return carry

    def transfers(i, carry):
        e_ref[rows_at(256 + i * 256, 256), :] = turned(g_ref[groups + i])
        return carry

    lax.fori_loop(0, groups, bases, 0, unroll=2)
    lax.fori_loop(0, g_ref.shape[0] - groups, transfers, 0, unroll=2)


def field_kernel(
    rank,
    leaf_dev,
    size,
    near_pos,
    far_pos,
    xb_hbm,
    xo_hbm,
    xa_hbm,
    gb_hbm,
    ga_hbm,
    b_hbm,
    s_hbm,
    e_hbm,
    basis_hbm,
    coeff_hbm,
    down_hbm,
    out_ref,
    xs,
    gb,
    ga,
    b_ref,
    s_ref,
    e_ref,
    basis_ref,
    win,
    down,
    sems,
):
    depth = leaf_dev.bit_length() - 1
    rows = leaf_dev * size
    offset = {k: 3 * (2**k - 8) * rank for k in range(3, depth + 1)}
    copies = []

    def begin(src, dst):
        copies.append(pltpu.make_async_copy(src, dst, sems.at[len(copies)]))
        copies[-1].start()
        return copies[-1]

    first = [
        begin(gb_hbm, gb),
        begin(ga_hbm, ga),
        begin(xb_hbm, xs.at[pl.ds(0, rows)]),
        begin(xa_hbm, xs.at[pl.ds(2 * rows, rows)]),
    ]
    second = [begin(down_hbm, down.at[pl.ds(0, 4 * rank)]), begin(s_hbm, s_ref), begin(e_hbm, e_ref)]
    for k in range(3, depth + 1):
        level = 2**k * rank
        second.append(
            begin(
                coeff_hbm.at[pl.ds((2**k - 8) * rank, level)], win.at[pl.ds(offset[k] + level, level)]
            )
        )
    third = [
        begin(xo_hbm, xs.at[pl.ds(rows, rows)]),
        begin(basis_hbm, basis_ref),
        begin(b_hbm, b_ref),
    ]
    total = 3 * (2 ** (depth + 1) - 8) * rank
    win[total : total + rank, :] = jnp.zeros((rank, win.shape[1]), BF)
    xs[3 * rows : 3 * rows + size, :] = jnp.zeros((size, xs.shape[1]), BF)
    for copy in first:
        copy.wait()
    after = {k: offset[k] + 2 * 2**k * rank for k in offset}
    up_pass([(xs, 0, gb, offset), (xs, 2 * rows, ga, after)], win, rank, leaf_dev)
    for copy in second:
        copy.wait()
    slots = s_ref.shape[2] // rank
    for k in range(3, depth + 1):

        def group(i, carry, k=k):
            parents = down[rows_at((2 ** (k - 1) - 4) * rank + i * 128, 128), :]
            base = (2**k - 8) + i * 8
            total_now = dot(e_ref[rows_at(base * rank, 256), :], parents)
            fars = []
            for j in range(8):
                node = base + j
                parts = [
                    win[rows_at(far_pos[node * slots + s] * rank, rank), :] for s in range(slots)
                ]
                fars.append(dot(s_ref[node + 7], jnp.concatenate(parts, axis=0)))
            total_now = total_now + jnp.concatenate(fars, axis=0)
            down[rows_at((2**k - 4) * rank + i * 256, 256), :] = total_now.astype(BF)
            return carry

        lax.fori_loop(0, 2**k // 8, group, 0)
    for copy in third:
        copy.wait()
    near_slots = b_ref.shape[2] // size

    def leaves(i, carry):
        state = down[rows_at((2**depth - 4) * rank + i * 128, 128), :]
        here = rows_at(i * 256, 256)
        near = []
        for j in range(4):
            leaf = i * 4 + j
            parts = [
                xs[rows_at(near_pos[leaf * near_slots + s] * size, size), :]
                for s in range(near_slots)
            ]
            near.append(dot(b_ref[leaf], jnp.concatenate(parts, axis=0)))
        out = jnp.concatenate(near, axis=0) + dot(basis_ref[here, :], state)
        out_ref[here, :] = out.astype(BF)
        return carry

    lax.fori_loop(0, leaf_dev // 4, leaves, 0, unroll=2)


def grouped_up(transfer):
    count, rank = transfer.shape[0], transfer.shape[1]
    return transfer.reshape(count // 8, 8, rank, rank).transpose(0, 3, 1, 2).reshape(-1, rank, 8 * rank)


def shards(
    points,
    leaf_basis,
    local_transfer,
    top_transfer,
    local_coupling,
    local_lists,
    top_coupling,
    top_lists,
    near_blocks,
    near_lists,
):
    leaf_dev, size, rank = leaf_basis.shape
    vecs = points.shape[1]
    depth = leaf_dev.bit_length() - 1
    devices = lax.axis_size("leaf")
    top_depth = devices.bit_length() - 1
    own = lax.axis_index("leaf")
    up = [(i, i + 1) for i in range(devices - 1)]
    back = [(i + 1, i) for i in range(devices - 1)]

    x_before = lax.ppermute(points, "leaf", up)
    x_after = lax.ppermute(points, "leaf", back)
    basis_up = (
        leaf_basis.reshape(leaf_dev // 4, 4, size, rank)
        .transpose(0, 3, 1, 2)
        .reshape(leaf_dev // 4, rank, 4 * size)
    )
    g_own = jnp.concatenate([basis_up, grouped_up(local_transfer[15:])], axis=0)
    g_before = lax.ppermute(g_own, "leaf", up)
    g_after = lax.ppermute(g_own, "leaf", back)

    def padded(rows):
        flat = rows.transpose(2, 0, 1).reshape(rank, -1)
        return jnp.pad(flat, ((0, 0), (0, 256 - flat.shape[1])))

    low_up = jnp.stack(
        [padded(local_transfer[a:b]) for a, b in ((7, 15), (3, 7), (1, 3), (0, 1))]
    )
    nodes = 2 * leaf_dev - 8
    coeff_own, root_term = pl.pallas_call(
        functools.partial(own_kernel, rank, leaf_dev),
        out_shape=(
            jax.ShapeDtypeStruct((nodes * rank, vecs), BF),
            jax.ShapeDtypeStruct((rank, vecs), F32),
        ),
        in_specs=[VMEM] * 3,
        out_specs=(VMEM, VMEM),
        compiler_params=PARAMS,
        cost_estimate=pl.CostEstimate(flops=600_000_000, bytes_accessed=5_000_000, transcendentals=0),
        name="own_up",
    )(points, g_own, low_up)
    steps = jnp.arange(2, top_depth)
    ancestors = (devices + own) >> (top_depth - steps)
    lists = top_lists[ancestors]
    top_pos = jnp.where(lists >= 0, lists, 0).reshape(-1)
    s_top = top_coupling[ancestors].transpose(0, 2, 1, 3).reshape(top_depth - 2, rank, -1)
    e_top = top_transfer[ancestors]
    low_down = local_transfer[:8].reshape(8 * rank, rank)
    up_top = grouped_up(top_transfer[8:])
    first_leaf = (own - 1) * leaf_dev
    near_pos = jnp.where(near_lists >= 0, near_lists - first_leaf, 3 * leaf_dev).reshape(-1)
    far_lists = local_lists[7:]
    row = jnp.arange(7, 2 * leaf_dev - 1)
    width = jnp.zeros_like(row)
    for k in range(3, depth + 1):
        width = jnp.where(row >= 2**k - 1, 2**k, width)
    start = 3 * (width - 8) - (own - 1) * width
    far_pos = jnp.where(far_lists >= 0, far_lists + start[:, None], 3 * nodes).reshape(-1)
    other = lax.ppermute(root_term, "leaf", [(i, i ^ 1) for i in range(devices)])
    gathered = (root_term + other).astype(BF)
    for bit in range(1, top_depth):
        flip = 2**bit
        if bit == 1:
            near_blocks, local_coupling, g_late, gathered = lax.optimization_barrier(
                (near_blocks, local_coupling, g_own, gathered)
            )
        other = lax.ppermute(gathered, "leaf", [(i, i ^ flip) for i in range(devices)])
        if bit == 1:
            near_cat = near_blocks.transpose(0, 2, 1, 3).reshape(leaf_dev, size, -1)
            near_cat = with_layout_constraint(near_cat, Layout((0, 1, 2)))
            s_cat = local_coupling.transpose(0, 2, 1, 3).reshape(2 * leaf_dev - 1, rank, -1)
            s_cat = with_layout_constraint(s_cat, Layout((0, 1, 2)))
            e_groups, basis_groups = pl.pallas_call(
                prep_kernel,
                out_shape=(
                    jax.ShapeDtypeStruct((nodes * rank, 4 * rank), BF),
                    jax.ShapeDtypeStruct((leaf_dev * size, 4 * rank), BF),
                ),
                in_specs=[VMEM] * 2,
                out_specs=(VMEM, VMEM),
                compiler_params=PARAMS,
                cost_estimate=pl.CostEstimate(flops=400_000_000, bytes_accessed=5_000_000, transcendentals=0),
                name="prepare_down",
            )(g_late, low_up)
            near_cat, s_cat, e_groups, basis_groups, other = lax.optimization_barrier(
                (near_cat, s_cat, e_groups, basis_groups, other)
            )
            g_before, g_after, other = lax.optimization_barrier(
                (g_before, g_after, other)
            )
            top_pos, s_top, e_top, up_top, low_down, near_pos, far_pos, other = (
                lax.optimization_barrier(
                    (top_pos, s_top, e_top, up_top, low_down, near_pos, far_pos, other)
                )
            )
        upper = (own & flip) > 0
        gathered = jnp.concatenate(
            [jnp.where(upper, other, gathered), jnp.where(upper, gathered, other)], axis=0
        )

    down_two = pl.pallas_call(
        functools.partial(top_kernel, rank, top_depth),
        out_shape=jax.ShapeDtypeStruct((4 * rank, vecs), BF),
        in_specs=[SMEM] + [VMEM] * 5,
        out_specs=VMEM,
        scratch_shapes=[pltpu.VMEM((devices * rank, vecs), BF)],
        compiler_params=PARAMS,
        cost_estimate=pl.CostEstimate(flops=50_000_000, bytes_accessed=1_000_000, transcendentals=0),
        name="top_tree",
    )(top_pos, gathered, up_top, s_top, e_top, low_down)

    any_space = pl.BlockSpec(memory_space=pl.ANY)
    return pl.pallas_call(
        functools.partial(field_kernel, rank, leaf_dev, size),
        out_shape=jax.ShapeDtypeStruct((leaf_dev * size, vecs), BF),
        in_specs=[SMEM] * 2 + [any_space] * 11,
        out_specs=VMEM,
        scratch_shapes=[
            pltpu.VMEM(((3 * leaf_dev + 1) * size, vecs), BF),
            pltpu.VMEM(g_own.shape, BF),
            pltpu.VMEM(g_own.shape, BF),
            pltpu.VMEM(near_cat.shape, BF),
            pltpu.VMEM(s_cat.shape, BF),
            pltpu.VMEM(e_groups.shape, BF),
            pltpu.VMEM(basis_groups.shape, BF),
            pltpu.VMEM(((3 * nodes + 1) * rank, vecs), BF),
            pltpu.VMEM(((nodes + 4) * rank, vecs), BF),
            pltpu.SemaphoreType.DMA((10 + depth - 2,)),
        ],
        compiler_params=PARAMS,
        cost_estimate=pl.CostEstimate(
            flops=4_000_000_000, bytes_accessed=30_000_000, transcendentals=0
        ),
        name="near_and_far",
    )(
        near_pos,
        far_pos,
        x_before,
        points,
        x_after,
        g_before,
        g_after,
        near_cat,
        s_cat,
        e_groups,
        basis_groups,
        coeff_own,
        down_two,
    )


def solution(mesh):
    return jax.shard_map(
        shards,
        mesh=mesh,
        in_specs=(
            P("leaf", None),
            P("leaf", None, None),
            P("leaf", None, None),
            P(),
            P("leaf", None, None, None),
            P("leaf", None),
            P(),
            P(),
            P("leaf", None, None, None),
            P("leaf", None),
        ),
        out_specs=P("leaf", None),
        check_vma=False,
    )
```
